128 devices in a mesh: amp: 16 (over y, z), blk: 8 (over x, core).
Axes of the slice: x: 4, y: 4, z: 4, core: 2. Of those that a mesh axis runs over, the one named last changes fastest.
Arguments:
- pixels: float32 [1048576, 512], P(('amp', 'blk')), may hold values from -24 to 24, as said below
- sketch: float32 [512, 128], replicated, may hold values from -0.25 to 0.25
Outputs:
- basis: float32 [1048576, 128], P(('amp', 'blk'))
- coefficients: float32 [512, 128], replicated
The draws below stay inside these ranges and needn't reach their ends.
Inputs may be any that keep to these rules, and one draw needn't show every extreme that they name: `pixels`: pixel values, finite.
All inputs are finite; a program needn't handle non-finite values.
Results may differ from the reference program's by a relative error of at most 0.0003.
Values sent between devices are 32-bit elements; how exact they have to be, the bound alone decides.
No kernel may reach another device: no remote copies, remote signals or barrier semaphores. Data moves between devices by JAX's collectives and lax.ppermute only.
A program may use at most 128 MiB of HBM per device.

```python
import jax
import jax.numpy as jnp
from jax import lax

F = 512
K = 128
POWER = 3
PIXELS = 1048576


def draw_pixels(key, part):
    key = jax.random.fold_in(key, 11)
    key_rows = jax.random.fold_in(key, 1)
    key_vals = jax.random.fold_in(key, 2)
    position = jnp.arange(PIXELS, dtype=jnp.float32) / PIXELS
    rough = 0.75 + 0.5 * jax.random.uniform(key_rows, (PIXELS,), jnp.float32)
    row_scale = jnp.exp(jnp.log(4.0) * position) * rough
    values = jax.random.normal(key_vals, (PIXELS, F), jnp.float32)
    return jnp.clip(row_scale[:, None] * values, -24.0, 24.0).astype(jnp.float32)


def noise(stream_key, shape, deviation, bound, held_as=jnp.bfloat16):
    return jnp.clip(deviation * jax.random.normal(stream_key, shape, jnp.float32), -bound, bound).astype(held_as)


def setup_inputs(seed: int = 0) -> dict:
    keys = jax.random.split(jax.random.key(seed), 3)
    return {
        "pixels": draw_pixels(jax.random.fold_in(keys[2], 71), 0),
        "sketch": noise(keys[1], (F, K), F ** -0.5, 0.25, jnp.float32),
    }


def reference(pixels, sketch):
    high = lax.Precision.HIGHEST
    current = jnp.dot(pixels.astype(jnp.float32), sketch.astype(jnp.float32), precision=high, preferred_element_type=jnp.float32)
    lower_factor = None
    mixed = None
    for sweep in range(POWER + 1):
        gram_block = jnp.dot(current.T.astype(jnp.float32), current.astype(jnp.float32), precision=high, preferred_element_type=jnp.float32)
        cross_block = jnp.dot(pixels.T.astype(jnp.float32), current.astype(jnp.float32), precision=high, preferred_element_type=jnp.float32)
        lower_factor = jnp.linalg.cholesky(gram_block)
        mixed = jax.scipy.linalg.solve_triangular(lower_factor, cross_block.T, lower=True).T
        if sweep < POWER:
            current = jnp.dot(pixels.astype(jnp.float32), mixed.astype(jnp.float32), precision=high, preferred_element_type=jnp.float32)
    scale = jnp.sqrt(jnp.asarray(PIXELS, dtype=pixels.dtype))
    coefficients = mixed / scale
    identity = jnp.eye(K, dtype=pixels.dtype)
    inverse = jax.scipy.linalg.solve_triangular(lower_factor, identity, lower=True).T * scale
    basis = jnp.dot(current.astype(jnp.float32), inverse.astype(jnp.float32), precision=high, preferred_element_type=jnp.float32)
    return (basis, coefficients)
```

```python
import jax
import jax.numpy as jnp
from jax import lax
from jax.experimental import pallas as pl
from jax.experimental.pallas import tpu as pltpu
from jax.sharding import PartitionSpec as P

POWER = 3
AXES = ("amp", "blk")
CHUNK = 1024
HALF = 256


def split(x):
    high = x.astype(jnp.bfloat16)
    return high, (x - high.astype(jnp.float32)).astype(jnp.bfloat16)


def dot_t(a, b):
    return lax.dot_general(a, b, (((0,), (0,)), ((), ())), preferred_element_type=jnp.float32)


def gram_kernel(x_ref, out_ref, hh_ref, hl_ref):
    step = pl.program_id(0)

    @pl.when(step == 0)
    def _():
        hh_ref[...] = jnp.zeros_like(hh_ref)
        hl_ref[...] = jnp.zeros_like(hl_ref)

    high, low = split(x_ref[...])
    left, right = high[:, :HALF], high[:, HALF:]
    hh_ref[0] += dot_t(left, left)
    hh_ref[1] += dot_t(left, right)
    hh_ref[2] += dot_t(right, right)
    hl_ref[...] += dot_t(high, low)

    @pl.when(step == pl.num_programs(0) - 1)
    def _():
        hl = hl_ref[...]
        both = hl + hl.T
        out_ref[0] = hh_ref[0] + both[:HALF, :HALF]
        out_ref[1] = hh_ref[1] + both[:HALF, HALF:]
        out_ref[2] = hh_ref[2] + both[HALF:, HALF:]


def gram(pixels):
    rows, frames = pixels.shape
    return pl.pallas_call(
        gram_kernel,
        grid=(rows // CHUNK,),
        in_specs=[pl.BlockSpec((CHUNK, frames), lambda i: (i, 0))],
        out_specs=pl.BlockSpec((3, HALF, HALF), lambda i: (0, 0, 0)),
        out_shape=jax.ShapeDtypeStruct((3, HALF, HALF), jnp.float32),
        scratch_shapes=[
            pltpu.VMEM((3, HALF, HALF), jnp.float32),
            pltpu.VMEM((frames, frames), jnp.float32),
        ],
        compiler_params=pltpu.CompilerParams(vmem_limit_bytes=48 * 2**20),
    )(pixels)


def basis_kernel(x_ref, b_ref, out_ref):
    b_high, b_low = split(b_ref[...])
    both = jnp.concatenate([b_high, b_low], axis=1)
    high, low = split(x_ref[...])
    wide = jnp.dot(high, both, preferred_element_type=jnp.float32)
    rank = out_ref.shape[1]
    out_ref[...] = wide[:, :rank] + wide[:, rank:] + jnp.dot(low, b_high, preferred_element_type=jnp.float32)


def apply_basis(pixels, matrix):
    rows, frames = pixels.shape
    rank = matrix.shape[1]
    return pl.pallas_call(
        basis_kernel,
        grid=(rows // CHUNK,),
        in_specs=[
            pl.BlockSpec((CHUNK, frames), lambda i: (i, 0)),
            pl.BlockSpec((frames, rank), lambda i: (0, 0)),
        ],
        out_specs=pl.BlockSpec((CHUNK, rank), lambda i: (i, 0)),
        out_shape=jax.ShapeDtypeStruct((rows, rank), jnp.float32),
        compiler_params=pltpu.CompilerParams(vmem_limit_bytes=48 * 2**20),
    )(pixels, matrix)


def total(blocks):
    devices = lax.axis_size("amp") * lax.axis_size("blk")
    pieces = blocks.reshape(devices, -1, 128)
    pieces = lax.all_to_all(pieces, AXES, 0, 0, tiled=True)
    piece = jnp.sum(pieces, axis=0)
    pieces = jnp.broadcast_to(piece[None], (devices,) + piece.shape)
    pieces = lax.all_to_all(pieces, AXES, 0, 0, tiled=True)
    return pieces.reshape(blocks.shape)


def factor(gram_block, cross_block):
    lower_factor = jnp.linalg.cholesky(gram_block)
    mixed = jax.scipy.linalg.solve_triangular(lower_factor, cross_block.T, lower=True).T
    return (lower_factor, mixed)


def body(pixels, sketch):
    high = lax.Precision.HIGHEST
    rank = sketch.shape[1]
    pixel_count = pixels.shape[0] * lax.axis_size("amp") * lax.axis_size("blk")
    summed = total(gram(pixels))
    square = jnp.concatenate(
        [
            jnp.concatenate([summed[0], summed[1]], axis=1),
            jnp.concatenate([summed[1].T, summed[2]], axis=1),
        ],
        axis=0,
    )
    mixed = sketch
    lower_factor = None
    start = None
    for _ in range(POWER + 1):
        start = mixed
        cross_block = jnp.dot(square, start, precision=high, preferred_element_type=jnp.float32)
        gram_block = jnp.dot(start.T, cross_block, precision=high, preferred_element_type=jnp.float32)
        lower_factor, mixed = factor(gram_block, cross_block)
    scale = jnp.sqrt(jnp.asarray(pixel_count, dtype=pixels.dtype))
    coefficients = mixed / scale
    identity = jnp.eye(rank, dtype=pixels.dtype)
    inverse = jax.scipy.linalg.solve_triangular(lower_factor, identity, lower=True).T * scale
    matrix = jnp.dot(start, inverse, precision=high, preferred_element_type=jnp.float32)
    return (apply_basis(pixels, matrix), coefficients)


def solution(mesh):
    return jax.shard_map(
        body,
        mesh=mesh,
        in_specs=(P(AXES, None), P()),
        out_specs=(P(AXES, None), P()),
        check_vma=False,
    )
```

```python
import functools
import math

import jax
import jax.numpy as jnp
from jax import lax
from jax.experimental import pallas as pl
from jax.experimental.pallas import tpu as pltpu
from jax.sharding import PartitionSpec as P

POWER = 3
AXES = ("amp", "blk")
CHUNK = 1024
HALF = 256
SUB = 8


def split(x):
    high = x.astype(jnp.bfloat16)
    return high, (x - high.astype(jnp.float32)).astype(jnp.bfloat16)


def dot_t(a, b):
    return lax.dot_general(a, b, (((0,), (0,)), ((), ())), preferred_element_type=jnp.float32)


def gram_kernel(x_ref, out_ref, hh_ref, hl_ref):
    step = pl.program_id(0)

    @pl.when(step == 0)
    def _():
        hh_ref[...] = jnp.zeros_like(hh_ref)
        hl_ref[...] = jnp.zeros_like(hl_ref)

    high, low = split(x_ref[...])
    left, right = high[:, :HALF], high[:, HALF:]
    hh_ref[0] += dot_t(left, left)
    hh_ref[1] += dot_t(left, right)
    hh_ref[2] += dot_t(right, right)
    hl_ref[...] += dot_t(high, low)

    @pl.when(step == pl.num_programs(0) - 1)
    def _():
        hl = hl_ref[...]
        both = hl + hl.T
        out_ref[0] = hh_ref[0] + both[:HALF, :HALF]
        out_ref[1] = hh_ref[1] + both[:HALF, HALF:]
        out_ref[2] = hh_ref[2] + both[HALF:, HALF:]


def gram(pixels):
    rows, frames = pixels.shape
    return pl.pallas_call(
        gram_kernel,
        grid=(rows // CHUNK,),
        in_specs=[pl.BlockSpec((CHUNK, frames), lambda i: (i, 0))],
        out_specs=pl.BlockSpec((3, HALF, HALF), lambda i: (0, 0, 0)),
        out_shape=jax.ShapeDtypeStruct((3, HALF, HALF), jnp.float32),
        scratch_shapes=[
            pltpu.VMEM((3, HALF, HALF), jnp.float32),
            pltpu.VMEM((frames, frames), jnp.float32),
        ],
        compiler_params=pltpu.CompilerParams(vmem_limit_bytes=48 * 2**20),
    )(pixels)


def basis_kernel(x_ref, b_ref, out_ref):
    b_high, b_low = split(b_ref[...])
    both = jnp.concatenate([b_high, b_low], axis=1)
    high, low = split(x_ref[...])
    wide = jnp.dot(high, both, preferred_element_type=jnp.float32)
    rank = out_ref.shape[1]
    out_ref[...] = wide[:, :rank] + wide[:, rank:] + jnp.dot(low, b_high, preferred_element_type=jnp.float32)


def apply_basis(pixels, matrix):
    rows, frames = pixels.shape
    rank = matrix.shape[1]
    return pl.pallas_call(
        basis_kernel,
        grid=(rows // CHUNK,),
        in_specs=[
            pl.BlockSpec((CHUNK, frames), lambda i: (i, 0)),
            pl.BlockSpec((frames, rank), lambda i: (0, 0)),
        ],
        out_specs=pl.BlockSpec((CHUNK, rank), lambda i: (i, 0)),
        out_shape=jax.ShapeDtypeStruct((rows, rank), jnp.float32),
        compiler_params=pltpu.CompilerParams(vmem_limit_bytes=48 * 2**20),
    )(pixels, matrix)


def total(blocks):
    devices = lax.axis_size("amp") * lax.axis_size("blk")
    pieces = blocks.reshape(devices, -1, 128)
    pieces = lax.all_to_all(pieces, AXES, 0, 0, tiled=True)
    piece = jnp.sum(pieces, axis=0)
    pieces = jnp.broadcast_to(piece[None], (devices,) + piece.shape)
    pieces = lax.all_to_all(pieces, AXES, 0, 0, tiled=True)
    return pieces.reshape(blocks.shape)


def contract(a, b, dims):
    return lax.dot_general(
        a, b, (dims, ((), ())), precision=lax.Precision.HIGHEST, preferred_element_type=jnp.float32
    )


def lanes(block, at):
    return jnp.broadcast_to(block[:, at : at + 1], block.shape)


def subs(block, at):
    return jnp.broadcast_to(block[at : at + 1, :], block.shape)


def inverse_factor(a):
    n = a.shape[0]
    blocks = n // SUB
    row = lax.broadcasted_iota(jnp.int32, (SUB, n), 0)
    col = lax.broadcasted_iota(jnp.int32, (SUB, n), 1)
    left = [a[SUB * g : SUB * (g + 1), :] for g in range(blocks)]
    right = [(col == row + SUB * g).astype(jnp.float32) for g in range(blocks)]
    out = []
    for b in range(blocks):
        at = SUB * b
        cols = [lanes(left[b], at + j) for j in range(SUB)]
        s = {(i, j): subs(cols[j], i) for j in range(SUB) for i in range(j, SUB)}
        ra = [subs(left[b], j) for j in range(SUB)]
        rj = [subs(right[b], j) for j in range(SUB)]
        inv, f = [], {}
        for j in range(SUB):
            inv.append(1.0 / s[j, j])
            for i in range(j + 1, SUB):
                f[i, j] = s[i, j] * inv[j]
            for i in range(j + 1, SUB):
                for l in range(j + 1, i + 1):
                    s[i, l] = s[i, l] - f[i, j] * s[l, j]
            for i in range(j + 1, SUB):
                ra[i] = ra[i] - f[i, j] * ra[j]
                rj[i] = rj[i] - f[i, j] * rj[j]
        done = rj[SUB - 1] * lax.rsqrt(s[SUB - 1, SUB - 1])
        for j in range(SUB - 1):
            done = jnp.where(row == j, rj[j] * lax.rsqrt(s[j, j]), done)
        out.append(done)
        if b + 1 < blocks:
            za = [ra[j] * inv[j] for j in range(SUB)]
            zj = [rj[j] * inv[j] for j in range(SUB)]
            for j in range(SUB - 1, -1, -1):
                for i in range(j):
                    za[i] = za[i] - f[j, i] * za[j]
                    zj[i] = zj[i] - f[j, i] * zj[j]
            for g in range(b + 1, blocks):
                cols = [lanes(left[g], at + j) for j in range(SUB)]
                for j in range(SUB):
                    left[g] = left[g] - cols[j] * za[j]
                    right[g] = right[g] - cols[j] * zj[j]
    return jnp.concatenate(out, axis=0)


def rounds_kernel(scale, g_ref, sketch_ref, matrix_ref, coef_ref, mixed_ref, start_ref, inv_ref):
    mixed_ref[...] = sketch_ref[...]

    def step(_, carry):
        start = mixed_ref[...]
        top, bottom = start[:HALF], start[HALF:]
        cross_top = contract(g_ref[0], top, ((1,), (0,))) + contract(g_ref[1], bottom, ((1,), (0,)))
        cross_bottom = contract(g_ref[1], top, ((0,), (0,))) + contract(g_ref[2], bottom, ((1,), (0,)))
        gram_block = contract(top, cross_top, ((0,), (0,))) + contract(bottom, cross_bottom, ((0,), (0,)))
        inv = inverse_factor(gram_block)
        start_ref[...] = start
        inv_ref[...] = inv
        mixed_ref[:HALF] = contract(cross_top, inv, ((1,), (1,)))
        mixed_ref[HALF:] = contract(cross_bottom, inv, ((1,), (1,)))
        return carry

    lax.fori_loop(0, POWER + 1, step, 0)
    coef_ref[...] = mixed_ref[...] * (1.0 / scale)
    matrix_ref[...] = contract(start_ref[...], inv_ref[...], ((1,), (1,))) * scale


def rounds(blocks, sketch, scale):
    frames, rank = sketch.shape
    return pl.pallas_call(
        functools.partial(rounds_kernel, scale),
        out_shape=[jax.ShapeDtypeStruct((frames, rank), jnp.float32)] * 2,
        scratch_shapes=[
            pltpu.VMEM((frames, rank), jnp.float32),
            pltpu.VMEM((frames, rank), jnp.float32),
            pltpu.VMEM((rank, rank), jnp.float32),
        ],
        compiler_params=pltpu.CompilerParams(vmem_limit_bytes=48 * 2**20),
    )(blocks, sketch)


def body(pixels, sketch):
    pixel_count = pixels.shape[0] * lax.axis_size("amp") * lax.axis_size("blk")
    summed = total(gram(pixels))
    matrix, coefficients = rounds(summed, sketch, math.sqrt(pixel_count))
    return (apply_basis(pixels, matrix), coefficients)


def solution(mesh):
    return jax.shard_map(
        body,
        mesh=mesh,
        in_specs=(P(AXES, None), P()),
        out_specs=(P(AXES, None), P()),
        check_vma=False,
    )
```

```python
import functools
import math

import jax
import jax.numpy as jnp
from jax import lax
from jax.experimental import pallas as pl
from jax.experimental.pallas import tpu as pltpu
from jax.sharding import Mesh
from jax.sharding import PartitionSpec as P

POWER = 3
AXES = ("y", "z", "x", "core")
SIZES = (4, 4, 4, 2)
CHUNK = 1024
HALF = 256
SUB = 8
TILE = 128
PAIRS = tuple((i, j) for i in range(4) for j in range(i, 4))


def split(x):
    high = x.astype(jnp.bfloat16)
    return high, (x - high.astype(jnp.float32)).astype(jnp.bfloat16)


def dot_t(a, b):
    return lax.dot_general(a, b, (((0,), (0,)), ((), ())), preferred_element_type=jnp.float32)


def gram_kernel(x_ref, out_ref, hh_ref, hl_ref):
    step = pl.program_id(0)

    @pl.when(step == 0)
    def _():
        hh_ref[...] = jnp.zeros_like(hh_ref)
        hl_ref[...] = jnp.zeros_like(hl_ref)

    high, low = split(x_ref[...])
    left, right = high[:, :HALF], high[:, HALF:]
    hh_ref[0] += dot_t(left, left)
    hh_ref[1] += dot_t(left, right)
    hh_ref[2] += dot_t(right, right)
    hl_ref[...] += dot_t(high, low)

    @pl.when(step == pl.num_programs(0) - 1)
    def _():
        hl = hl_ref[...]
        both = hl + hl.T
        quarters = (
            hh_ref[0] + both[:HALF, :HALF],
            hh_ref[1] + both[:HALF, HALF:],
            hh_ref[2] + both[HALF:, HALF:],
        )
        for at, (i, j) in enumerate(PAIRS):
            quarter = quarters[i // 2 + j // 2]
            r, c = TILE * (i % 2), TILE * (j % 2)
            out_ref[TILE * at : TILE * (at + 1), :] = quarter[r : r + TILE, c : c + TILE]


def gram(pixels):
    rows, frames = pixels.shape
    return pl.pallas_call(
        gram_kernel,
        grid=(rows // CHUNK,),
        in_specs=[pl.BlockSpec((CHUNK, frames), lambda i: (i, 0))],
        out_specs=pl.BlockSpec((TILE * len(PAIRS), TILE), lambda i: (0, 0)),
        out_shape=jax.ShapeDtypeStruct((TILE * len(PAIRS), TILE), jnp.float32),
        scratch_shapes=[
            pltpu.VMEM((3, HALF, HALF), jnp.float32),
            pltpu.VMEM((frames, frames), jnp.float32),
        ],
        compiler_params=pltpu.CompilerParams(vmem_limit_bytes=48 * 2**20),
    )(pixels)


def basis_kernel(x_ref, b_ref, out_ref):
    b_high, b_low = split(b_ref[...])
    both = jnp.concatenate([b_high, b_low], axis=1)
    high, low = split(x_ref[...])
    wide = jnp.dot(high, both, preferred_element_type=jnp.float32)
    rank = out_ref.shape[1]
    out_ref[...] = wide[:, :rank] + wide[:, rank:] + jnp.dot(low, b_high, preferred_element_type=jnp.float32)


def apply_basis(pixels, matrix):
    rows, frames = pixels.shape
    rank = matrix.shape[1]
    return pl.pallas_call(
        basis_kernel,
        grid=(rows // CHUNK,),
        in_specs=[
            pl.BlockSpec((CHUNK, frames), lambda i: (i, 0)),
            pl.BlockSpec((frames, rank), lambda i: (0, 0)),
        ],
        out_specs=pl.BlockSpec((CHUNK, rank), lambda i: (i, 0)),
        out_shape=jax.ShapeDtypeStruct((rows, rank), jnp.float32),
        compiler_params=pltpu.CompilerParams(vmem_limit_bytes=48 * 2**20),
    )(pixels, matrix)


def all_to_all(pieces):
    return lax.all_to_all(pieces, ("y", "x"), 0, 0, tiled=True)


def swap(x, axis, bit):
    return lax.ppermute(x, axis, [(i, i ^ bit) for i in range(lax.axis_size(axis))])


def total(x):
    core = lax.axis_index("core")
    half = x.shape[0] // 2
    mine = lax.dynamic_slice_in_dim(x, core * half, half, 0)
    other = lax.dynamic_slice_in_dim(x, (1 - core) * half, half, 0)
    mine = mine + swap(other, "core", 1)
    group = lax.axis_size("y") * lax.axis_size("x")
    piece = jnp.sum(all_to_all(mine.reshape(group, -1, x.shape[1])), axis=0)
    for bit in (1, 3):
        piece = piece + swap(piece, "z", bit)
    mine = all_to_all(jnp.broadcast_to(piece[None], (group,) + piece.shape)).reshape(mine.shape)
    other = swap(mine, "core", 1)
    return jnp.where(core == 0, jnp.concatenate([mine, other]), jnp.concatenate([other, mine]))


def contract(a, b, dims):
    return lax.dot_general(
        a, b, (dims, ((), ())), precision=lax.Precision.HIGHEST, preferred_element_type=jnp.float32
    )


def lanes(block, at):
    return jnp.broadcast_to(block[:, at : at + 1], block.shape)


def subs(block, at):
    return jnp.broadcast_to(block[at : at + 1, :], block.shape)


def inverse_factor(a):
    n = a.shape[0]
    blocks = n // SUB
    row = lax.broadcasted_iota(jnp.int32, (SUB, n), 0)
    col = lax.broadcasted_iota(jnp.int32, (SUB, n), 1)
    left = [a[SUB * g : SUB * (g + 1), :] for g in range(blocks)]
    right = [(col == row + SUB * g).astype(jnp.float32) for g in range(blocks)]
    out = []
    for b in range(blocks):
        at = SUB * b
        cols = [lanes(left[b], at + j) for j in range(SUB)]
        s = {(i, j): subs(cols[j], i) for j in range(SUB) for i in range(j, SUB)}
        ra = [subs(left[b], j) for j in range(SUB)]
        rj = [subs(right[b], j) for j in range(SUB)]
        inv, f = [], {}
        for j in range(SUB):
            inv.append(1.0 / s[j, j])
            for i in range(j + 1, SUB):
                f[i, j] = s[i, j] * inv[j]
            for i in range(j + 1, SUB):
                for l in range(j + 1, i + 1):
                    s[i, l] = s[i, l] - f[i, j] * s[l, j]
            for i in range(j + 1, SUB):
                ra[i] = ra[i] - f[i, j] * ra[j]
                rj[i] = rj[i] - f[i, j] * rj[j]
        done = rj[SUB - 1] * lax.rsqrt(s[SUB - 1, SUB - 1])
        for j in range(SUB - 1):
            done = jnp.where(row == j, rj[j] * lax.rsqrt(s[j, j]), done)
        out.append(done)
        if b + 1 < blocks:
            za = [ra[j] * inv[j] for j in range(SUB)]
            zj = [rj[j] * inv[j] for j in range(SUB)]
            for j in range(SUB - 1, -1, -1):
                for i in range(j):
                    za[i] = za[i] - f[j, i] * za[j]
                    zj[i] = zj[i] - f[j, i] * zj[j]
            for g in range(b + 1, blocks):
                cols = [lanes(left[g], at + j) for j in range(SUB)]
                for j in range(SUB):
                    left[g] = left[g] - cols[j] * za[j]
                    right[g] = right[g] - cols[j] * zj[j]
    return jnp.concatenate(out, axis=0)


def rounds_kernel(scale, blocks_ref, sketch_ref, matrix_ref, coef_ref, g_ref, mixed_ref, start_ref, inv_ref):
    mixed_ref[...] = sketch_ref[...]
    for at, (i, j) in enumerate(PAIRS):
        block = blocks_ref[TILE * at : TILE * (at + 1), :]
        g_ref[TILE * i : TILE * (i + 1), TILE * j : TILE * (j + 1)] = block
        if i != j:
            g_ref[TILE * j : TILE * (j + 1), TILE * i : TILE * (i + 1)] = block.T

    def step(_, carry):
        start = mixed_ref[...]
        cross_block = contract(g_ref[...], start, ((1,), (0,)))
        gram_block = contract(start, cross_block, ((0,), (0,)))
        inv = inverse_factor(gram_block)
        start_ref[...] = start
        inv_ref[...] = inv
        mixed_ref[...] = contract(cross_block, inv, ((1,), (1,)))
        return carry

    lax.fori_loop(0, POWER + 1, step, 0)
    coef_ref[...] = mixed_ref[...] * (1.0 / scale)
    matrix_ref[...] = contract(start_ref[...], inv_ref[...], ((1,), (1,))) * scale


def rounds(blocks, sketch, scale):
    frames, rank = sketch.shape
    return pl.pallas_call(
        functools.partial(rounds_kernel, scale),
        out_shape=[jax.ShapeDtypeStruct((frames, rank), jnp.float32)] * 2,
        scratch_shapes=[
            pltpu.VMEM((frames, frames), jnp.float32),
            pltpu.VMEM((frames, rank), jnp.float32),
            pltpu.VMEM((frames, rank), jnp.float32),
            pltpu.VMEM((rank, rank), jnp.float32),
        ],
        compiler_params=pltpu.CompilerParams(vmem_limit_bytes=48 * 2**20),
    )(blocks, sketch)


def body(pixels, sketch):
    pixel_count = pixels.shape[0] * math.prod(SIZES)
    summed = total(gram(pixels))
    matrix, coefficients = rounds(summed, sketch, math.sqrt(pixel_count))
    return (apply_basis(pixels, matrix), coefficients)


def solution(mesh):
    return jax.shard_map(
        body,
        mesh=Mesh(mesh.devices.reshape(SIZES), AXES),
        in_specs=(P(AXES, None), P()),
        out_specs=(P(AXES, None), P()),
        check_vma=False,
    )
```

```python
import functools
import math

import jax
import jax.numpy as jnp
from jax import lax
from jax.experimental import pallas as pl
from jax.experimental.pallas import tpu as pltpu
from jax.sharding import Mesh
from jax.sharding import PartitionSpec as P

POWER = 3
AXES = ("y", "z", "x", "core")
SIZES = (4, 4, 4, 2)
CHUNK = 1024
HALF = 256
SUB = 8
AHEAD = 3
TILE = 128
PAIRS = tuple((i, j) for i in range(4) for j in range(i, 4))


def split(x):
    high = x.astype(jnp.bfloat16)
    return high, (x - high.astype(jnp.float32)).astype(jnp.bfloat16)


def dot_t(a, b):
    return lax.dot_general(a, b, (((0,), (0,)), ((), ())), preferred_element_type=jnp.float32)


def gram_kernel(x_ref, out_ref, hh_ref, hl_ref):
    step = pl.program_id(0)

    @pl.when(step == 0)
    def _():
        hh_ref[...] = jnp.zeros_like(hh_ref)
        hl_ref[...] = jnp.zeros_like(hl_ref)

    high, low = split(x_ref[...])
    left, right = high[:, :HALF], high[:, HALF:]
    hh_ref[0] += dot_t(left, left)
    hh_ref[1] += dot_t(left, right)
    hh_ref[2] += dot_t(right, right)
    hl_ref[...] += dot_t(high, low)

    @pl.when(step == pl.num_programs(0) - 1)
    def _():
        hl = hl_ref[...]
        both = hl + hl.T
        quarters = (
            hh_ref[0] + both[:HALF, :HALF],
            hh_ref[1] + both[:HALF, HALF:],
            hh_ref[2] + both[HALF:, HALF:],
        )
        for at, (i, j) in enumerate(PAIRS):
            quarter = quarters[i // 2 + j // 2]
            r, c = TILE * (i % 2), TILE * (j % 2)
            out_ref[TILE * at : TILE * (at + 1), :] = quarter[r : r + TILE, c : c + TILE]


def gram(pixels):
    rows, frames = pixels.shape
    return pl.pallas_call(
        gram_kernel,
        grid=(rows // CHUNK,),
        in_specs=[pl.BlockSpec((CHUNK, frames), lambda i: (i, 0))],
        out_specs=pl.BlockSpec((TILE * len(PAIRS), TILE), lambda i: (0, 0)),
        out_shape=jax.ShapeDtypeStruct((TILE * len(PAIRS), TILE), jnp.float32),
        scratch_shapes=[
            pltpu.VMEM((3, HALF, HALF), jnp.float32),
            pltpu.VMEM((frames, frames), jnp.float32),
        ],
        compiler_params=pltpu.CompilerParams(vmem_limit_bytes=48 * 2**20),
    )(pixels)


def all_to_all(pieces):
    return lax.all_to_all(pieces, ("y", "x"), 0, 0, tiled=True)


def swap(x, axis, bit):
    return lax.ppermute(x, axis, [(i, i ^ bit) for i in range(lax.axis_size(axis))])


def total(x):
    core = lax.axis_index("core")
    half = x.shape[0] // 2
    mine = lax.dynamic_slice_in_dim(x, core * half, half, 0)
    other = lax.dynamic_slice_in_dim(x, (1 - core) * half, half, 0)
    mine = mine + swap(other, "core", 1)
    group = lax.axis_size("y") * lax.axis_size("x")
    piece = jnp.sum(all_to_all(mine.reshape(group, -1, x.shape[1])), axis=0)
    for bit in (1, 3):
        piece = piece + swap(piece, "z", bit)
    mine = all_to_all(jnp.broadcast_to(piece[None], (group,) + piece.shape)).reshape(mine.shape)
    other = swap(mine, "core", 1)
    return jnp.where(core == 0, jnp.concatenate([mine, other]), jnp.concatenate([other, mine]))


def thirds(x):
    high = x.astype(jnp.bfloat16)
    rest = x - high.astype(jnp.float32)
    mid, low = split(rest)
    return high, mid, low


def contract(a, b, dims):
    return lax.dot_general(a, b, (dims, ((), ())), preferred_element_type=jnp.float32)


def lanes(block, at):
    return jnp.broadcast_to(block[:, at : at + 1], block.shape)


def rank_update(scaled, rows):
    h1, m1, l1 = (p.astype(jnp.float32) for p in thirds(scaled))
    h2, m2, l2 = (p.astype(jnp.float32) for p in thirds(rows))
    first = jnp.concatenate([h1, h1, m1, h1, m1, l1], axis=0).astype(jnp.bfloat16)
    second = jnp.concatenate([h2, m2, h2, l2, m2, h2], axis=0).astype(jnp.bfloat16)
    return contract(first, second, ((0,), (0,)))


def inverse_factor(a, buf_ref):
    n = a.shape[0]
    blocks = n // SUB
    row = lax.broadcasted_iota(jnp.int32, (SUB, n), 0)
    col = lax.broadcasted_iota(jnp.int32, (SUB, n), 1)
    rows = [a[SUB * g : SUB * (g + 1), :] for g in range(blocks)]
    out = []
    for b in range(blocks):
        at, slot = SUB * b, b % 2
        panel = (col >= at) & (col < at + SUB)
        own = rows[b]
        for j in range(SUB):
            buf_ref[slot, j] = lanes(own, at + j)
        s = {
            (i, j): jnp.broadcast_to(buf_ref[slot, j, i : i + 1, :], (SUB, n))
            for j in range(SUB)
            for i in range(j, SUB)
        }
        own = jnp.where(panel, (col == row + at).astype(jnp.float32), own)
        r = [jnp.broadcast_to(own[j : j + 1, :], own.shape) for j in range(SUB)]
        near = range(b + 1, min(b + 1 + AHEAD, blocks))
        columns = {}
        for g in near:
            columns[g] = [lanes(rows[g], at + j) for j in range(SUB)]
            rows[g] = jnp.where(panel, 0.0, rows[g])
        inv, f = [], {}
        for j in range(SUB):
            inv.append(1.0 / s[j, j])
            for i in range(j + 1, SUB):
                f[i, j] = s[i, j] * inv[j]
            for i in range(j + 1, SUB):
                for l in range(j + 1, i + 1):
                    s[i, l] = s[i, l] - f[i, j] * s[l, j]
            for i in range(j + 1, SUB):
                r[i] = r[i] - f[i, j] * r[j]
                for g in near:
                    columns[g][i] = columns[g][i] - f[i, j] * columns[g][j]
            for g in near:
                rows[g] = rows[g] - (columns[g][j] * inv[j]) * r[j]
        done, pivot, inverse = r[-1], s[SUB - 1, SUB - 1], inv[-1]
        for j in range(SUB - 1):
            done = jnp.where(row == j, r[j], done)
            pivot = jnp.where(row == j, s[j, j], pivot)
            inverse = jnp.where(row == j, inv[j], inverse)
        out.append(jnp.where(col < at + SUB, done * lax.rsqrt(pivot), 0.0))
        far = range(b + 1 + AHEAD, blocks)
        if far:
            update = rank_update(done * inverse, done)
            for g in far:
                rows[g] = jnp.where(panel, 0.0, rows[g]) - update[SUB * g : SUB * (g + 1), :]
    return jnp.concatenate(out, axis=0)


def times_inverse(x, inv):
    xh, xm, xl = thirds(x)
    ih, im, il = thirds(inv)
    first = jnp.concatenate([xh, xh, xm, xh, xl, xm], axis=1)
    second = jnp.concatenate([ih, im, ih, il, ih, im], axis=1)
    return contract(first, second, ((1,), (1,)))


def finish_kernel(
    scale, blocks_ref, sketch_ref, x_ref, basis_ref, coef_ref, g_ref, mixed_ref, start_ref, inv_ref, buf_ref,
    held_ref, done_ref, in_sems, out_sems,
):
    rows = x_ref.shape[0]
    chunks = rows // CHUNK

    def fetch(i):
        at = pl.ds(pl.multiple_of(i * CHUNK, CHUNK), CHUNK)
        return pltpu.make_async_copy(x_ref.at[at], held_ref.at[at], in_sems.at[i])

    def store(i):
        at = pl.ds(pl.multiple_of(i * CHUNK, CHUNK), CHUNK)
        return pltpu.make_async_copy(done_ref.at[at], basis_ref.at[at], out_sems.at[i])

    for i in range(chunks):
        fetch(i).start()

    frames, rank = sketch_ref.shape
    mixed_ref[...] = sketch_ref[...]
    for at, (i, j) in enumerate(PAIRS):
        block = blocks_ref[TILE * at : TILE * (at + 1), :]
        for p, q in ((i, j), (j, i))[: 1 if i == j else 2]:
            part = thirds(block if (p, q) == (i, j) else block.T)
            for k in range(3):
                g_ref[TILE * p : TILE * (p + 1), k * frames + TILE * q : k * frames + TILE * (q + 1)] = part[k]

    def step(_, carry):
        start = mixed_ref[...]
        sh, sm, sl = thirds(start)
        pair = jnp.concatenate([sh, sm], axis=1)
        high = contract(g_ref[:, :frames], pair, ((1,), (0,)))
        mid = contract(g_ref[:, frames : 2 * frames], pair, ((1,), (0,)))
        small = contract(g_ref[:, :frames], sl, ((1,), (0,))) + contract(g_ref[:, 2 * frames :], sh, ((1,), (0,)))
        cross = high[:, :rank] + ((high[:, rank:] + mid[:, :rank]) + (mid[:, rank:] + small))
        ch, cm, cl = thirds(cross)
        square = contract(pair, jnp.concatenate([ch, cm], axis=1), ((0,), (0,)))
        small = contract(sh, cl, ((0,), (0,))) + contract(sl, ch, ((0,), (0,)))
        gram_block = square[:rank, :rank] + (
            (square[:rank, rank:] + square[rank:, :rank]) + (square[rank:, rank:] + small)
        )
        inv = inverse_factor(gram_block, buf_ref)
        start_ref[...] = start
        inv_ref[...] = inv
        mixed_ref[...] = times_inverse(cross, inv)
        return carry

    lax.fori_loop(0, POWER + 1, step, 0)
    coef_ref[...] = mixed_ref[...] * (1.0 / scale)
    b_high, b_low = split(times_inverse(start_ref[...], inv_ref[...]) * scale)
    both = jnp.concatenate([b_high, b_low], axis=1)

    def apply(i, carry):
        fetch(i).wait()
        at = pl.ds(pl.multiple_of(i * CHUNK, CHUNK), CHUNK)
        high, low = split(held_ref[at, :])
        wide = contract(high, both, ((1,), (0,)))
        done_ref[at, :] = wide[:, :rank] + (wide[:, rank:] + contract(low, b_high, ((1,), (0,))))
        store(i).start()
        return carry

    lax.fori_loop(0, chunks, apply, 0)
    for i in range(chunks):
        store(i).wait()


def finish(blocks, sketch, pixels, scale):
    frames, rank = sketch.shape
    rows = pixels.shape[0]
    whole = pl.BlockSpec(memory_space=pltpu.VMEM)
    outside = pl.BlockSpec(memory_space=pl.ANY)
    return pl.pallas_call(
        functools.partial(finish_kernel, scale),
        in_specs=[whole, whole, outside],
        out_specs=[outside, whole],
        out_shape=[
            jax.ShapeDtypeStruct((rows, rank), jnp.float32),
            jax.ShapeDtypeStruct((frames, rank), jnp.float32),
        ],
        scratch_shapes=[
            pltpu.VMEM((frames, 3 * frames), jnp.bfloat16),
            pltpu.VMEM((frames, rank), jnp.float32),
            pltpu.VMEM((frames, rank), jnp.float32),
            pltpu.VMEM((rank, rank), jnp.float32),
            pltpu.VMEM((2, SUB, SUB, rank), jnp.float32),
            pltpu.VMEM((rows, frames), jnp.float32),
            pltpu.VMEM((rows, rank), jnp.float32),
            pltpu.SemaphoreType.DMA((rows // CHUNK,)),
            pltpu.SemaphoreType.DMA((rows // CHUNK,)),
        ],
        compiler_params=pltpu.CompilerParams(vmem_limit_bytes=48 * 2**20),
    )(blocks, sketch, pixels)


def body(pixels, sketch):
    pixel_count = pixels.shape[0] * math.prod(SIZES)
    summed = total(gram(pixels))
    return finish(summed, sketch, pixels, math.sqrt(pixel_count))


def solution(mesh):
    return jax.shard_map(
        body,
        mesh=Mesh(mesh.devices.reshape(SIZES), AXES),
        in_specs=(P(AXES, None), P()),
        out_specs=(P(AXES, None), P()),
        check_vma=False,
    )
```
